32 devices in a mesh: loc: 4 (over z), ev: 8 (over y, x, core).
Axes of the slice: x: 2, y: 2, z: 4, core: 2. Of those that a mesh axis runs over, the one named last changes fastest.
Arguments:
- damage_noise: bfloat16 [1024, 32768], P('ev', 'loc'), may hold values from -4 to 4
- insured_value: float32 [32768], P('loc'), may hold values from 0.1 to 1
- policy_id: int32 [32768], P('loc'), may hold values from 0 to 4095
- bands: int32 [1024, 2], P('ev'), may hold values from 0 to 32768, as said below
- peak: float32 [1024], P('ev'), may hold values from 2 to 6
- event_year: int32 [1024], P('ev'), may hold values from 0 to 255, as said below
- deductible: float32 [4096], replicated, may hold values from 0.05 to 0.5
- limit: float32 [4096], replicated, may hold values from 0.5 to 2
- levels: int32 [32], replicated, may hold values from 0 to 149
Outputs:
- annual_loss: float32 [256], P('ev')
- occurrence_loss: float32 [256], P('ev')
- aggregate_curve: float32 [32], replicated
- occurrence_curve: float32 [32], replicated
The draws below stay inside these ranges and needn't reach their ends.
Inputs may be any that keep to these rules, and one draw needn't show every extreme that they name: bands[e,0] < bands[e,1]; each band spans 2048 to 16384 locations. `event_year`: among the 128 events of one index of ev, at most 32 have years in any one index's block of 32 years (years j * 32 to (j + 1) * 32 - 1); in every draw some block of years receives exactly 32 events from every index of ev.
All inputs are finite; a program needn't handle non-finite values.
Results may differ from the reference program's by a relative error of at most 0.0003.
Values sent between devices are 32-bit elements; how exact they have to be, the bound alone decides.
A program may use at most 64 MiB of HBM per device.

```python
import math
import jax
import jax.numpy as jnp
from jax import lax

L_DEV = 8192
EV_DEV = 128
YR_DEV = 32
POLICIES = 4096
LEVELS = 32
CAP = 32
LOCS = 32768
EVENTS = 1024
YEARS = 256


def draw_bands(key, part):
    block_count = LOCS // L_DEV
    key_width, key_start, key_kind, key_cover, key_first, key_rim = jax.random.split(key, 6)
    band_width = jax.random.randint(key_width, (EVENTS,), LOCS // 16, LOCS // 2 + 1)
    band_start = jax.random.randint(key_start, (EVENTS,), 0, LOCS - band_width + 1)
    fewest_blocks = (block_count + 15) // 16
    most_blocks = max(fewest_blocks, block_count // 2 - 1 - block_count // 32)
    covered = jax.random.randint(key_cover, (EVENTS,), fewest_blocks, most_blocks + 1)
    first_block = jax.random.randint(key_first, (EVENTS,), 1, block_count - covered)
    rim_rate = jax.random.randint(key_rim, (EVENTS,), 27, 36)
    rim_size = covered * L_DEV * rim_rate // 1000
    aligned_low = jnp.maximum(first_block * L_DEV - rim_size, 0)
    aligned_high = jnp.minimum((first_block + covered) * L_DEV + rim_size, LOCS)
    aligned = jax.random.randint(key_kind, (EVENTS,), 0, 4) < 3
    band_low = jnp.where(aligned, aligned_low, band_start)
    band_high = jnp.where(aligned, aligned_high, band_start + band_width)
    return jnp.stack([band_low, band_high], axis=1).astype(jnp.int32)


def draw_event_year(key, part):
    owner_count = EVENTS // EV_DEV
    pool_size = owner_count * CAP
    pool = jnp.repeat(jnp.arange(owner_count, dtype=jnp.int32), CAP)
    key_common, key_blocks, key_years = jax.random.split(key, 3)
    common = jax.random.randint(key_common, (), 0, owner_count)

    def one_block(block_key):
        key_second, key_scores, key_order = jax.random.split(block_key, 3)
        second = jax.random.randint(key_second, (), 0, owner_count)
        scores = jax.random.randint(key_scores, (pool_size,), 0, 65536) * pool_size + jnp.arange(pool_size, dtype=jnp.int32)
        tier = jnp.where(pool == common, 0, jnp.where(pool == second, 1, 2))
        ordered = pool[jnp.argsort(tier * (65536 * pool_size) + scores)]
        chosen = ordered[:EV_DEV]
        return chosen[jax.random.permutation(key_order, EV_DEV)]
    owners = jax.vmap(one_block)(jax.random.split(key_blocks, owner_count)).reshape(EVENTS)
    return (owners * YR_DEV + jax.random.randint(key_years, (EVENTS,), 0, YR_DEV)).astype(jnp.int32)


def set_ends(result, key, low, top_value):
    longest = result.shape.index(max(result.shape))
    spots = []
    for shift in (0, 1):
        where = [jax.random.randint(jax.random.fold_in(key, axis), (), 0, length) for axis, length in enumerate(result.shape)]
        where[longest] = (where[longest] + shift) % result.shape[longest]
        spots.append(tuple(where))
    return result.at[spots[0]].set(low).at[spots[1]].set(top_value)


def block_levels(rng, shape, pieces, low, high):
    def one(dim, parts):
        heights = jax.random.uniform(jax.random.fold_in(jax.random.fold_in(rng, 6), dim), (parts,), jnp.float32, low / len(pieces), high / len(pieces))
        return jnp.repeat(jnp.exp(heights), shape[dim] // parts).reshape((-1,) + (1,) * (len(shape) - dim - 1))

    gain = one(*pieces[0])
    for cut in pieces[1:]:
        gain = gain * one(*cut)
    return gain


def centred(own_key, extent, deviation, most, shards=(), kind=jnp.bfloat16):
    entries = deviation * jax.random.normal(own_key, extent, jnp.float32)
    if shards:
        entries = entries * block_levels(own_key, extent, shards, -0.22, 0.18)
    return jnp.clip(entries, -most, most).astype(kind)


def setup_inputs(seed: int = 0) -> dict:
    keys = jax.random.split(jax.random.key(seed), 10)
    damage_noise = centred(keys[0], (EVENTS, LOCS), 1.0, 4.0, ((0, 8), (1, 4)))
    insured_value = jnp.clip(jnp.exp(math.log(1.0) - 2.3025851 * jax.random.uniform(keys[1], (LOCS,), jnp.float32) ** block_levels(keys[1], (LOCS,), ((0, 4),), -0.2, 0.2)), 0.1, 1.0)
    policy_id = set_ends(jax.random.randint(keys[2], (LOCS,), 0, POLICIES), jax.random.fold_in(keys[2], 1), 0, POLICIES - 1).astype(jnp.int32)
    bands = draw_bands(jax.random.fold_in(keys[9], 71), 0)
    peak = jnp.clip(jnp.exp(math.log(6.0) - 1.0986123 * jax.random.uniform(keys[4], (EVENTS,), jnp.float32) ** block_levels(keys[4], (EVENTS,), ((0, 8),), -0.2, 0.2)), 2.0, 6.0)
    event_year = draw_event_year(jax.random.fold_in(keys[9], 71), 0)
    deductible = jnp.clip(jnp.exp(jax.random.uniform(keys[6], (POLICIES,), jnp.float32, math.log(0.05), math.log(0.5))), 0.05, 0.5)
    limit = jnp.clip(jnp.exp(jax.random.uniform(keys[7], (POLICIES,), jnp.float32, math.log(0.5), math.log(2.0))), 0.5, 2.0)
    levels = set_ends(jax.random.randint(keys[8], (LEVELS,), 0, 150), jax.random.fold_in(keys[8], 1), 0, 149).astype(jnp.int32)
    return dict(damage_noise=damage_noise, insured_value=insured_value, policy_id=policy_id, bands=bands, peak=peak, event_year=event_year, deductible=deductible, limit=limit, levels=levels)


def ground_losses(damage_noise, insured_value, bands, peak, anchor):
    amount = insured_value.shape[0]
    position = (anchor + lax.iota(jnp.int32, amount)).astype(jnp.float32) + 0.5
    band_low = bands[:, 0].astype(jnp.float32)
    band_high = bands[:, 1].astype(jnp.float32)
    center = 0.5 * (band_low + band_high)
    half_width = 0.5 * (band_high - band_low)
    offset = (position[None, :] - center[:, None]) / half_width[:, None]
    wind_speed = peak[:, None] * jnp.maximum(1.0 - offset * offset, 0.0)
    cube_wind = wind_speed * wind_speed * wind_speed
    damage_ratio = cube_wind / (cube_wind + 1.0)
    factor = jnp.exp(0.5 * damage_noise.astype(jnp.float32) - 0.125)
    return (insured_value[None, :] * damage_ratio * factor).astype(jnp.bfloat16)


def excess(losses, thresholds):
    return jnp.mean(jnp.maximum(losses[:, None] - thresholds[None, :], 0.0), axis=0)


def reference(damage_noise, insured_value, policy_id, bands, peak, event_year, deductible, limit, levels):
    block_size = min(1024, LOCS)

    def accumulate(block_index, running):
        offset_start = (block_index * block_size).astype(jnp.int32)
        noise_block = lax.dynamic_slice_in_dim(damage_noise, offset_start, block_size, 1)
        value_block = lax.dynamic_slice_in_dim(insured_value, offset_start, block_size, 0)
        owner_block = lax.dynamic_slice_in_dim(policy_id, offset_start, block_size, 0)
        ground = ground_losses(noise_block, value_block, bands, peak, offset_start)
        return running + jax.ops.segment_sum(ground.astype(jnp.float32).T, owner_block, num_segments=POLICIES)

    gross = lax.fori_loop(0, LOCS // block_size, accumulate, jnp.zeros((POLICIES, EVENTS), jnp.float32))
    net = jnp.minimum(jnp.maximum(gross - deductible[:, None], 0.0), limit[:, None])
    event_loss = jnp.sum(net, axis=0) / POLICIES
    annual_loss = jax.ops.segment_sum(event_loss, event_year, num_segments=YEARS)
    occurrence_loss = jnp.maximum(jax.ops.segment_max(event_loss, event_year, num_segments=YEARS), 0.0)
    thresholds = levels.astype(jnp.float32) / 100.0
    return annual_loss, occurrence_loss, excess(annual_loss, thresholds), excess(occurrence_loss, thresholds)
```

```python
import functools

import jax
import jax.numpy as jnp
from jax import lax
from jax.experimental import pallas as pl
from jax.experimental.pallas import tpu as pltpu
from jax.sharding import PartitionSpec as P

YR_DEV = 32
LANES = 128
LOW = 256
GROUP = 16
CHUNK = 1024
LAG = 1


def kernel(
    axes, noise, insured, policy, bands, peak, year, deductible, limit, levels,
    annual_out, occurrence_out, aggregate_out, excess_out,
    block_mask, column_mask, center, inverse, strength, own, arrived, net_sum, halves, rows,
    annual_all, occurrence_all,
    send_sem, recv_sem, half_send, half_recv, row_send, row_recv,
):
    depth, owners = axes
    z = lax.axis_index("loc")
    ev = lax.axis_index("ev")
    events, locations = noise.shape
    policies = deductible.shape[0] * LANES
    blocks = policies // LOW
    half_blocks = blocks // 2
    groups = events // GROUP
    chunks = locations // CHUNK
    half_rows = half_blocks * GROUP

    barrier = pltpu.get_barrier_semaphore()
    for k in range(1, depth):
        pl.semaphore_signal(barrier, inc=1, device_id={"loc": lax.rem(z + k, depth)})
    for k in range(1, owners):
        pl.semaphore_signal(barrier, inc=1, device_id={"ev": lax.rem(ev + k, owners)})

    low = jnp.transpose(jnp.broadcast_to(bands[0:1, :].astype(jnp.float32), (LANES, events)))
    high = jnp.transpose(jnp.broadcast_to(bands[1:2, :].astype(jnp.float32), (LANES, events)))
    center[...] = 0.5 * (low + high)
    inverse[...] = 1.0 / (0.5 * (high - low))
    strength[...] = jnp.transpose(jnp.broadcast_to(peak[...], (LANES, events)))

    def build(c, carry):
        at = pl.ds(pl.multiple_of(c * CHUNK, CHUNK), CHUNK)
        ids = policy[:, at]
        column = jnp.broadcast_to(ids & (LOW - 1), (LOW, CHUNK))
        wanted = lax.broadcasted_iota(jnp.int32, (LOW, CHUNK), 0)
        column_mask[:, at] = jnp.where(column == wanted, 1.0, 0.0).astype(jnp.bfloat16)
        block = jnp.broadcast_to(ids >> 8, (GROUP, CHUNK))
        for b in range(blocks):
            block_mask[b * GROUP : (b + 1) * GROUP, at] = jnp.where(block == b, 1.0, 0.0).astype(
                jnp.bfloat16
            )
        return carry

    lax.fori_loop(0, chunks, build, 0)
    pl.semaphore_wait(barrier, depth - 1 + owners - 1)

    anchor = z * locations
    wide = CHUNK // LANES

    def compute(g):
        which = pl.ds(pl.multiple_of(g * GROUP, GROUP), GROUP)
        mid = jnp.concatenate([center[which, :]] * wide, axis=1)
        inv = jnp.concatenate([inverse[which, :]] * wide, axis=1)
        top = jnp.concatenate([strength[which, :]] * wide, axis=1)

        def part(c, total):
            start = pl.multiple_of(c * CHUNK, CHUNK)
            at = pl.ds(start, CHUNK)
            place = lax.broadcasted_iota(jnp.int32, (GROUP, CHUNK), 1) + (anchor + start)
            offset = (place.astype(jnp.float32) + 0.5 - mid) * inv
            wind = top * jnp.maximum(1.0 - offset * offset, 0.0)
            cube = wind * wind * wind
            factor = jnp.exp(0.5 * noise[which, at].astype(jnp.float32) - 0.125)
            ground = (insured[:, at] * (cube / (cube + 1.0)) * factor).astype(jnp.bfloat16)
            left = jnp.concatenate([ground] * blocks, axis=0) * block_mask[:, at]
            return total + lax.dot_general(
                left, column_mask[:, at], (((1,), (1,)), ((), ())),
                preferred_element_type=jnp.float32,
            )

        total = lax.fori_loop(0, chunks, part, jnp.zeros((blocks * GROUP, LOW), jnp.float32))
        own[0, g] = total[:half_rows]
        own[1, g] = total[half_rows:]

    def hop(d, g, there):
        return pltpu.make_async_remote_copy(
            src_ref=own.at[d, g], dst_ref=arrived.at[d, g],
            send_sem=send_sem.at[d, g], recv_sem=recv_sem.at[d, g],
            device_id={"loc": there},
        )

    def settle(d, g):
        total = jnp.zeros((GROUP, LANES), jnp.float32)
        for b in range(half_blocks):
            for j in range(LOW // LANES):
                row = (d * half_blocks + b) * (LOW // LANES) + j
                gross = own[d, g, b * GROUP : (b + 1) * GROUP, j * LANES : (j + 1) * LANES]
                net = jnp.maximum(gross - deductible[row : row + 1, :], 0.0)
                total = total + jnp.minimum(net, limit[row : row + 1, :])
        net_sum[pl.ds(pl.multiple_of(g * GROUP, GROUP), GROUP), :] = total

    def step(s, carry):
        @pl.when(s < groups)
        def _():
            compute(s)

        for d in (0, 1):
            gone = z if d == 1 else depth - 1 - z
            there = jnp.minimum(z + 1, depth - 1) if d == 1 else jnp.maximum(z - 1, 0)
            g = s - LAG * gone
            active = (g >= 0) & (g < groups)

            @pl.when(active & (gone > 0))
            def _():
                hop(d, g, there).wait_recv()
                own[d, g] = own[d, g] + arrived[d, g]

            @pl.when(active & (gone < depth - 1))
            def _():
                hop(d, g, there).start()

            @pl.when(active & (gone == depth - 1))
            def _():
                settle(d, g)

        return carry

    lax.fori_loop(0, groups + LAG * (depth - 1), step, 0)

    def half_copy(d, k):
        return pltpu.make_async_remote_copy(
            src_ref=halves.at[d], dst_ref=halves.at[d],
            send_sem=half_send.at[k], recv_sem=half_recv.at[d],
            device_id={"loc": lax.rem(z + k, depth)},
        )

    for d in (0, 1):
        owner = 0 if d == 0 else depth - 1

        @pl.when(z == owner)
        def _():
            row = jnp.sum(jnp.transpose(net_sum[...]), axis=0, keepdims=True)
            halves[d] = jnp.broadcast_to(row, (8, events))
            for k in range(1, depth):
                half_copy(d, k).start()

    for d in (0, 1):
        owner = 0 if d == 0 else depth - 1

        @pl.when(z != owner)
        def _():
            half_copy(d, 1).wait_recv()

    loss = (halves[0] + halves[1]) / policies
    first = lax.broadcasted_iota(jnp.int32, (8, events), 0) == 0
    rows[ev] = jnp.where(first, loss, jnp.broadcast_to(year[...].astype(jnp.float32), (8, events)))

    def row_copy(k, slot):
        return pltpu.make_async_remote_copy(
            src_ref=rows.at[slot], dst_ref=rows.at[slot],
            send_sem=row_send.at[k], recv_sem=row_recv.at[k],
            device_id={"ev": lax.rem(ev + k, owners)},
        )

    for k in range(1, owners):
        row_copy(k, ev).start()
    for k in range(1, owners):
        row_copy(k, lax.rem(ev - k + owners, owners)).wait_recv()

    years = YR_DEV * owners
    span = 64
    threshold = levels[...].astype(jnp.float32) / 100.0

    def tally(c, sums):
        start = pl.multiple_of(c * span, span)
        label = (lax.broadcasted_iota(jnp.int32, (span, events), 0) + start).astype(jnp.float32)
        annual = jnp.zeros((span, events), jnp.float32)
        largest = jnp.zeros((span, events), jnp.float32)
        for r in range(owners):
            block = rows[r]
            hit = jnp.where(label == block[1:2, :], block[0:1, :], 0.0)
            annual = annual + hit
            largest = jnp.maximum(largest, hit)
        annual = jnp.sum(annual, axis=1, keepdims=True)
        largest = jnp.max(largest, axis=1, keepdims=True)
        annual_all[pl.ds(start, span), :] = jnp.broadcast_to(annual, (span, LANES))
        occurrence_all[pl.ds(start, span), :] = jnp.broadcast_to(largest, (span, LANES))
        return (
            sums[0] + jnp.sum(jnp.maximum(annual - threshold, 0.0), axis=0, keepdims=True),
            sums[1] + jnp.sum(jnp.maximum(largest - threshold, 0.0), axis=0, keepdims=True),
        )

    zero = jnp.zeros(levels.shape, jnp.float32)
    sums = lax.fori_loop(0, years // span, tally, (zero, zero))
    aggregate_out[...] = sums[0] / years
    excess_out[...] = sums[1] / years

    mine = pl.ds(pl.multiple_of(ev * YR_DEV, YR_DEV), YR_DEV)
    diagonal = lax.broadcasted_iota(jnp.int32, (YR_DEV, LANES), 0) == lax.broadcasted_iota(
        jnp.int32, (YR_DEV, LANES), 1
    )
    for out, every in ((annual_out, annual_all), (occurrence_out, occurrence_all)):
        row = jnp.sum(jnp.where(diagonal, every[mine, :], 0.0), axis=0, keepdims=True)
        out[...] = row[:, :YR_DEV]

    def drain(g, carry):
        for d in (0, 1):
            gone = z if d == 1 else depth - 1 - z

            @pl.when(gone < depth - 1)
            def _():
                hop(d, g, jnp.minimum(z + 1, depth - 1) if d == 1 else jnp.maximum(z - 1, 0)).wait_send()

        return carry

    lax.fori_loop(0, groups, drain, 0)
    for d in (0, 1):
        owner = 0 if d == 0 else depth - 1

        @pl.when(z == owner)
        def _():
            for k in range(1, depth):
                half_copy(d, k).wait_send()

    for k in range(1, owners):
        row_copy(k, ev).wait_send()


def local(
    damage_noise, insured_value, policy_id, bands, peak, event_year, deductible, limit, levels
):
    depth, owners = lax.axis_size("loc"), lax.axis_size("ev")
    events, locations = damage_noise.shape
    policies = deductible.shape[0]
    thresholds = levels.shape[0]
    blocks = policies // LOW
    groups = events // GROUP
    half_rows = blocks // 2 * GROUP
    years = YR_DEV * owners
    row = jax.ShapeDtypeStruct((1, YR_DEV), jnp.float32)
    curve = jax.ShapeDtypeStruct((1, thresholds), jnp.float32)
    vmem = pl.BlockSpec(memory_space=pltpu.VMEM)
    outs = pl.pallas_call(
        functools.partial(kernel, (depth, owners)),
        out_shape=(row, row, curve, curve),
        in_specs=[vmem] * 9,
        out_specs=(vmem,) * 4,
        scratch_shapes=[
            pltpu.VMEM((blocks * GROUP, locations), jnp.bfloat16),
            pltpu.VMEM((LOW, locations), jnp.bfloat16),
            pltpu.VMEM((events, LANES), jnp.float32),
            pltpu.VMEM((events, LANES), jnp.float32),
            pltpu.VMEM((events, LANES), jnp.float32),
            pltpu.VMEM((2, groups, half_rows, LOW), jnp.float32),
            pltpu.VMEM((2, groups, half_rows, LOW), jnp.float32),
            pltpu.VMEM((events, LANES), jnp.float32),
            pltpu.VMEM((2, 8, events), jnp.float32),
            pltpu.VMEM((owners, 8, events), jnp.float32),
            pltpu.VMEM((years, LANES), jnp.float32),
            pltpu.VMEM((years, LANES), jnp.float32),
            pltpu.SemaphoreType.DMA((2, groups)),
            pltpu.SemaphoreType.DMA((2, groups)),
            pltpu.SemaphoreType.DMA((depth,)),
            pltpu.SemaphoreType.DMA((2,)),
            pltpu.SemaphoreType.DMA((owners,)),
            pltpu.SemaphoreType.DMA((owners,)),
        ],
        compiler_params=pltpu.CompilerParams(
            collective_id=0, has_side_effects=True, vmem_limit_bytes=48 * 1024 * 1024
        ),
    )(
        damage_noise,
        insured_value.reshape(1, locations),
        policy_id.reshape(1, locations),
        bands.T,
        peak.reshape(1, events),
        event_year.reshape(1, events),
        deductible.reshape(policies // LANES, LANES),
        limit.reshape(policies // LANES, LANES),
        levels.reshape(1, thresholds),
    )
    return tuple(out.reshape(-1) for out in outs)


def solution(mesh):
    placed = (P("ev", "loc"), P("loc"), P("loc"), P("ev", None), P("ev"), P("ev"), P(), P(), P())
    return jax.shard_map(
        local, mesh=mesh, in_specs=placed, out_specs=(P("ev"), P("ev"), P(), P()), check_vma=False
    )
```

```python
import functools

import jax
import jax.numpy as jnp
from jax import lax
from jax.experimental import pallas as pl
from jax.experimental.pallas import tpu as pltpu
from jax.sharding import PartitionSpec as P

YR_DEV = 32
LANES = 128
LOW = 256
GROUP = 16
CHUNK = 4096
SPLIT = 2
LAG = 3


def kernel(
    axes, *refs
):
    sources, (result,), inputs, rest = refs[:9], refs[9:10], refs[10:19], refs[19:]
    noise, insured, policy, bands, peak, year, deductible, limit, levels = inputs
    (
        block_mask, column_mask, center, inverse, strength, own, arrived, net_sum, halves, rows,
        annual_all, occurrence_all,
        send_sem, recv_sem, half_send, half_recv, row_send, row_recv, load_sem,
    ) = rest
    depth, owners = axes
    z = lax.axis_index("loc")
    ev = lax.axis_index("ev")
    events, locations = noise.shape
    policies = deductible.shape[0] * LANES
    blocks = policies // LOW
    half_blocks = blocks // 2
    groups = events // GROUP
    chunks = locations // CHUNK
    piece_blocks = half_blocks // SPLIT
    piece_rows = piece_blocks * GROUP
    pieces = groups * SPLIT

    loads = [
        pltpu.make_async_copy(source, target, load_sem.at[i])
        for i, (source, target) in enumerate(zip(sources, inputs))
    ]
    for i in (2, 3, 4, 0, 1, 5, 6, 7, 8):
        loads[i].start()

    barrier = pltpu.get_barrier_semaphore()
    for k in range(1, depth):
        pl.semaphore_signal(barrier, inc=1, device_id={"loc": lax.rem(z + k, depth)})
    for k in range(1, owners):
        pl.semaphore_signal(barrier, inc=1, device_id={"ev": lax.rem(ev + k, owners)})

    for i in (2, 3, 4):
        loads[i].wait()
    low = jnp.transpose(jnp.broadcast_to(bands[0:1, :].astype(jnp.float32), (LANES, events)))
    high = jnp.transpose(jnp.broadcast_to(bands[1:2, :].astype(jnp.float32), (LANES, events)))
    center[...] = 0.5 * (low + high)
    inverse[...] = 1.0 / (0.5 * (high - low))
    strength[...] = jnp.transpose(jnp.broadcast_to(peak[...], (LANES, events)))

    def build(c, carry):
        at = pl.ds(pl.multiple_of(c * CHUNK, CHUNK), CHUNK)
        ids = policy[:, at]
        column = jnp.broadcast_to(ids & (LOW - 1), (LOW, CHUNK))
        wanted = lax.broadcasted_iota(jnp.int32, (LOW, CHUNK), 0)
        column_mask[:, at] = jnp.where(column == wanted, 1.0, 0.0).astype(jnp.bfloat16)
        block = jnp.broadcast_to(ids >> 8, (GROUP, CHUNK))
        for b in range(blocks):
            block_mask[b * GROUP : (b + 1) * GROUP, at] = jnp.where(block == b, 1.0, 0.0).astype(
                jnp.bfloat16
            )
        return carry

    lax.fori_loop(0, chunks, build, 0)
    for i in (0, 1, 5, 6, 7, 8):
        loads[i].wait()
    pl.semaphore_wait(barrier, depth - 1 + owners - 1)

    anchor = z * locations
    wide = CHUNK // LANES

    def compute(g):
        which = pl.ds(pl.multiple_of(g * GROUP, GROUP), GROUP)
        mid = jnp.concatenate([center[which, :]] * wide, axis=1)
        inv = jnp.concatenate([inverse[which, :]] * wide, axis=1)
        top = jnp.concatenate([strength[which, :]] * wide, axis=1)

        def part(c, total):
            start = pl.multiple_of(c * CHUNK, CHUNK)
            at = pl.ds(start, CHUNK)
            place = lax.broadcasted_iota(jnp.int32, (GROUP, CHUNK), 1) + (anchor + start)
            offset = (place.astype(jnp.float32) + 0.5 - mid) * inv
            wind = top * jnp.maximum(1.0 - offset * offset, 0.0)
            cube = wind * wind * wind
            factor = jnp.exp(0.5 * noise[which, at].astype(jnp.float32) - 0.125)
            ground = (insured[:, at] * (cube / (cube + 1.0)) * factor).astype(jnp.bfloat16)
            left = jnp.concatenate([ground] * blocks, axis=0) * block_mask[:, at]
            return total + lax.dot_general(
                left, column_mask[:, at], (((1,), (1,)), ((), ())),
                preferred_element_type=jnp.float32,
            )

        total = lax.fori_loop(0, chunks, part, jnp.zeros((blocks * GROUP, LOW), jnp.float32))
        for d in (0, 1):
            for j in range(SPLIT):
                top_row = (d * SPLIT + j) * piece_rows
                own[d, g * SPLIT + j] = total[top_row : top_row + piece_rows]

    def hop(d, g, there):
        return pltpu.make_async_remote_copy(
            src_ref=own.at[d, g], dst_ref=arrived.at[d, g],
            send_sem=send_sem.at[d, g], recv_sem=recv_sem.at[d, g],
            device_id={"loc": there},
        )

    def settle(d, j, q):
        total = jnp.zeros((GROUP, LANES), jnp.float32)
        for b in range(piece_blocks):
            for i in range(LOW // LANES):
                row = ((d * SPLIT + j) * piece_blocks + b) * (LOW // LANES) + i
                gross = own[d, q, b * GROUP : (b + 1) * GROUP, i * LANES : (i + 1) * LANES]
                net = jnp.maximum(gross - deductible[row : row + 1, :], 0.0)
                total = total + jnp.minimum(net, limit[row : row + 1, :])
        at = pl.multiple_of((q // SPLIT) * GROUP, GROUP)
        net_sum[j, pl.ds(at, GROUP), :] = total

    def step(s, carry):
        @pl.when(s < groups)
        def _():
            compute(s)

        for j in range(SPLIT):
            for d in (0, 1):
                gone = z if d == 1 else depth - 1 - z
                there = jnp.minimum(z + 1, depth - 1) if d == 1 else jnp.maximum(z - 1, 0)
                q = s * SPLIT + j - LAG * gone
                active = (q >= 0) & (q < pieces)

                @pl.when(active & (gone > 0))
                def _():
                    hop(d, q, there).wait_recv()
                    own[d, q] = own[d, q] + arrived[d, q]

                @pl.when(active & (gone < depth - 1))
                def _():
                    hop(d, q, there).start()

                @pl.when(active & (gone == depth - 1))
                def _():
                    settle(d, (j - LAG * (depth - 1)) % SPLIT, q)

        return carry

    lax.fori_loop(0, groups + (LAG * (depth - 1) + SPLIT - 1) // SPLIT, step, 0)

    def half_copy(d, k):
        return pltpu.make_async_remote_copy(
            src_ref=halves.at[d], dst_ref=halves.at[d],
            send_sem=half_send.at[k], recv_sem=half_recv.at[d],
            device_id={"loc": lax.rem(z + k, depth)},
        )

    for d in (0, 1):
        owner = 0 if d == 0 else depth - 1

        @pl.when(z == owner)
        def _():
            row = jnp.sum(jnp.transpose(sum(net_sum[j] for j in range(SPLIT))), axis=0, keepdims=True)
            halves[d] = jnp.broadcast_to(row, (8, events))
            for k in range(1, depth):
                half_copy(d, k).start()

    for d in (0, 1):
        owner = 0 if d == 0 else depth - 1

        @pl.when(z != owner)
        def _():
            half_copy(d, 1).wait_recv()

    loss = (halves[0] + halves[1]) / policies
    first = lax.broadcasted_iota(jnp.int32, (8, events), 0) == 0
    rows[ev] = jnp.where(first, loss, jnp.broadcast_to(year[...].astype(jnp.float32), (8, events)))

    def row_copy(k, slot):
        return pltpu.make_async_remote_copy(
            src_ref=rows.at[slot], dst_ref=rows.at[slot],
            send_sem=row_send.at[k], recv_sem=row_recv.at[k],
            device_id={"ev": lax.rem(ev + k, owners)},
        )

    for k in range(1, owners):
        row_copy(k, ev).start()
    for k in range(1, owners):
        row_copy(k, lax.rem(ev - k + owners, owners)).wait_recv()

    years = YR_DEV * owners
    span = 64
    threshold = levels[...].astype(jnp.float32) / 100.0

    def tally(c, sums):
        start = pl.multiple_of(c * span, span)
        label = (lax.broadcasted_iota(jnp.int32, (span, events), 0) + start).astype(jnp.float32)
        annual = jnp.zeros((span, events), jnp.float32)
        largest = jnp.zeros((span, events), jnp.float32)
        for r in range(owners):
            block = rows[r]
            hit = jnp.where(label == block[1:2, :], block[0:1, :], 0.0)
            annual = annual + hit
            largest = jnp.maximum(largest, hit)
        annual = jnp.sum(annual, axis=1, keepdims=True)
        largest = jnp.max(largest, axis=1, keepdims=True)
        annual_all[pl.ds(start, span), :] = jnp.broadcast_to(annual, (span, LANES))
        occurrence_all[pl.ds(start, span), :] = jnp.broadcast_to(largest, (span, LANES))
        return (
            sums[0] + jnp.sum(jnp.maximum(annual - threshold, 0.0), axis=0, keepdims=True),
            sums[1] + jnp.sum(jnp.maximum(largest - threshold, 0.0), axis=0, keepdims=True),
        )

    zero = jnp.zeros(levels.shape, jnp.float32)
    sums = lax.fori_loop(0, years // span, tally, (zero, zero))
    result[2:3, : levels.shape[1]] = sums[0] / years
    result[3:4, : levels.shape[1]] = sums[1] / years

    mine = pl.ds(pl.multiple_of(ev * YR_DEV, YR_DEV), YR_DEV)
    diagonal = lax.broadcasted_iota(jnp.int32, (YR_DEV, LANES), 0) == lax.broadcasted_iota(
        jnp.int32, (YR_DEV, LANES), 1
    )
    for i, every in enumerate((annual_all, occurrence_all)):
        row = jnp.sum(jnp.where(diagonal, every[mine, :], 0.0), axis=0, keepdims=True)
        result[i : i + 1, :] = row

    def drain(g, carry):
        for d in (0, 1):
            gone = z if d == 1 else depth - 1 - z

            @pl.when(gone < depth - 1)
            def _():
                hop(d, g, jnp.minimum(z + 1, depth - 1) if d == 1 else jnp.maximum(z - 1, 0)).wait_send()

        return carry

    lax.fori_loop(0, pieces, drain, 0)
    for d in (0, 1):
        owner = 0 if d == 0 else depth - 1

        @pl.when(z == owner)
        def _():
            for k in range(1, depth):
                half_copy(d, k).wait_send()

    for k in range(1, owners):
        row_copy(k, ev).wait_send()


def local(
    damage_noise, insured_value, policy_id, bands, peak, event_year, deductible, limit, levels
):
    depth, owners = lax.axis_size("loc"), lax.axis_size("ev")
    events, locations = damage_noise.shape
    policies = deductible.shape[0]
    thresholds = levels.shape[0]
    blocks = policies // LOW
    groups = events // GROUP
    pieces = groups * SPLIT
    piece_rows = blocks // 2 // SPLIT * GROUP
    years = YR_DEV * owners
    operands = (
        damage_noise,
        insured_value.reshape(1, locations),
        policy_id.reshape(1, locations),
        bands.T,
        peak.reshape(1, events),
        event_year.reshape(1, events),
        deductible.reshape(policies // LANES, LANES),
        limit.reshape(policies // LANES, LANES),
        levels.reshape(1, thresholds),
    )
    out = pl.pallas_call(
        functools.partial(kernel, (depth, owners)),
        out_shape=jax.ShapeDtypeStruct((8, LANES), jnp.float32),
        in_specs=[pl.BlockSpec(memory_space=pltpu.HBM)] * 9,
        out_specs=pl.BlockSpec(memory_space=pltpu.VMEM),
        scratch_shapes=[pltpu.VMEM(operand.shape, operand.dtype) for operand in operands]
        + [
            pltpu.VMEM((blocks * GROUP, locations), jnp.bfloat16),
            pltpu.VMEM((LOW, locations), jnp.bfloat16),
            pltpu.VMEM((events, LANES), jnp.float32),
            pltpu.VMEM((events, LANES), jnp.float32),
            pltpu.VMEM((events, LANES), jnp.float32),
            pltpu.VMEM((2, pieces, piece_rows, LOW), jnp.float32),
            pltpu.VMEM((2, pieces, piece_rows, LOW), jnp.float32),
            pltpu.VMEM((SPLIT, events, LANES), jnp.float32),
            pltpu.VMEM((2, 8, events), jnp.float32),
            pltpu.VMEM((owners, 8, events), jnp.float32),
            pltpu.VMEM((years, LANES), jnp.float32),
            pltpu.VMEM((years, LANES), jnp.float32),
            pltpu.SemaphoreType.DMA((2, pieces)),
            pltpu.SemaphoreType.DMA((2, pieces)),
            pltpu.SemaphoreType.DMA((depth,)),
            pltpu.SemaphoreType.DMA((2,)),
            pltpu.SemaphoreType.DMA((owners,)),
            pltpu.SemaphoreType.DMA((owners,)),
            pltpu.SemaphoreType.DMA((9,)),
        ],
        compiler_params=pltpu.CompilerParams(
            collective_id=0, has_side_effects=True, vmem_limit_bytes=62 * 1024 * 1024
        ),
    )(*operands)
    return out[0, :YR_DEV], out[1, :YR_DEV], out[2, :thresholds], out[3, :thresholds]


def solution(mesh):
    placed = (P("ev", "loc"), P("loc"), P("loc"), P("ev", None), P("ev"), P("ev"), P(), P(), P())
    return jax.shard_map(
        local, mesh=mesh, in_specs=placed, out_specs=(P("ev"), P("ev"), P(), P()), check_vma=False
    )
```
